32 devices in a mesh: freq: 4 (over z), rcv: 8 (over y, x, core).
Axes of the slice: x: 2, y: 2, z: 4, core: 2. Of those that a mesh axis runs over, the one named last changes fastest.
Arguments:
- reflection: bfloat16 [2, 96, 2048, 2048], P(None, 'freq', 'rcv'), may hold values from -0.4375 to 0.4375
- direct: float32 [24, 2048, 512], P('freq', 'rcv'), may hold values from -6 to 6
- onset_index: int32 [24, 2048], P('freq', 'rcv'), may hold values from 128 to 511
Outputs:
- focusing_plus: float32 [24, 2048, 512], P('freq', 'rcv')
- focusing_minus: float32 [24, 2048, 512], P('freq', 'rcv')
The draws below stay inside these ranges and needn't reach their ends.
All inputs are finite; a program needn't handle non-finite values.
Results may differ from the reference program's by a relative error of at most 0.024.
Values may be sent and summed in bfloat16 or wider, within the bound.
A program may use at most 192 MiB of HBM per device.

```python
import math
import jax
import jax.numpy as jnp
from jax import lax

S = 2048
NF = 96
NT = 512
FLO = 8
NP = 24
ITERS = 3


def place_ends(values, rng, low, largest):
    dims = values.shape
    place = [jax.random.randint(jax.random.fold_in(rng, axis), (), 0, dims[axis]) for axis in range(len(dims))]
    values = values.at[tuple(place)].set(low)
    longest = dims.index(max(dims))
    place[longest] = (place[longest] + 1) % dims[longest]
    return values.at[tuple(place)].set(largest)


def spiked(values, rng, source, target, blocks, factor):
    def block_of(dim):
        return (jnp.arange(values.shape[dim]) // (values.shape[dim] // blocks)).reshape((-1,) + (1,) * (values.ndim - 1 - dim))

    one_side = jax.random.permutation(rng, blocks)[block_of(target)]
    other_side = (block_of(target) + blocks // 2) % blocks
    return jnp.where((block_of(source) == one_side) | (block_of(source) == other_side), factor * values, values)


def level_of(stream_key, shape, cuts, smallest, high):
    gain = 1.0
    for axis_at, parts in cuts:
        heights = jax.random.uniform(jax.random.fold_in(jax.random.fold_in(stream_key, 6), axis_at), (parts,), jnp.float32, smallest / len(cuts), high / len(cuts))
        gain = gain * jnp.repeat(jnp.exp(heights), shape[axis_at] // parts).reshape((-1,) + (1,) * (len(shape) - 1 - axis_at))
    return gain


def normal_values(own_key, shape, deviation, limit, cuts=(), kind=jnp.bfloat16):
    loudness = level_of(own_key, shape, cuts, -0.22, 0.18) if cuts else 1.0
    drawn = jax.random.normal(own_key, shape, jnp.float32) * deviation * loudness
    return jnp.minimum(jnp.maximum(drawn, -limit), limit).astype(kind)


def bell_draw_with(own_key, dims, deviation, bound, split, heavy, held_as=jnp.bfloat16):
    result = deviation * jax.random.normal(own_key, dims, jnp.float32)
    if split:
        result = result * level_of(own_key, dims, split, -0.22, 0.18)
    return jnp.clip(spiked(result, jax.random.fold_in(own_key, 3), *heavy), -bound, bound).astype(held_as)


def setup_inputs(seed: int = 0) -> dict:
    key_list = jax.random.split(jax.random.key(seed), 4)
    return {
        "reflection": bell_draw_with(key_list[0], (2, NF, S, S), (0.4 * (NT / (NF * S)) ** 0.5), 0.4375, ((1, 4), (2, 8)), (2, 3, 8, 2.0)),
        "direct": normal_values(key_list[1], (NP, S, NT), 1.0, 6.0, ((0, 4), (1, 8)), jnp.float32),
        "onset_index": place_ends(jax.random.randint(key_list[2], (NP, S), NT // 4, NT), jax.random.fold_in(key_list[2], 1), NT // 4, NT - 1).astype(jnp.int32),
    }


def tables():
    samples = jnp.arange(NT, dtype=jnp.int32)
    bins = FLO + jnp.arange(NF, dtype=jnp.int32)
    phase = (bins[:, None] * samples[None, :]) % NT
    angles = phase.astype(jnp.float32) * (2.0 * math.pi / NT)
    return jnp.cos(angles), jnp.sin(angles)


def to_spectrum(field, cosine, sine_table):
    highest = lax.Precision.HIGHEST
    real_part = jnp.einsum('ft,pst->fps', cosine, field, precision=highest)
    imag_part = -jnp.einsum('ft,pst->fps', sine_table, field, precision=highest)
    return jnp.stack([real_part, imag_part]).astype(jnp.bfloat16)


def to_time(fourier_spectrum, cosine, sine_table):
    highest = lax.Precision.HIGHEST
    values = fourier_spectrum.astype(jnp.float32)
    first = jnp.einsum('ft,fps->pst', cosine, values[0], precision=highest)
    second = jnp.einsum('ft,fps->pst', sine_table, values[1], precision=highest)
    return (2.0 / NT) * (first - second)


def forward_apply(reflection, fourier_spectrum):
    def single(inputs):
        reflectivity_real, reflectivity_imaginary, spectral_real, spectral_imaginary = inputs
        real_part = jnp.dot(spectral_real, reflectivity_real.T, preferred_element_type=jnp.float32) - jnp.dot(spectral_imaginary, reflectivity_imaginary.T, preferred_element_type=jnp.float32)
        imag_part = jnp.dot(spectral_imaginary, reflectivity_real.T, preferred_element_type=jnp.float32) + jnp.dot(spectral_real, reflectivity_imaginary.T, preferred_element_type=jnp.float32)
        return jnp.stack([real_part, imag_part]).astype(jnp.bfloat16)
    stacked = lax.map(single, (reflection[0], reflection[1], fourier_spectrum[0], fourier_spectrum[1]))
    return jnp.transpose(stacked, (1, 0, 2, 3))


def adjoint_apply(reflection, fourier_spectrum):
    def single(inputs):
        reflectivity_real, reflectivity_imaginary, spectral_real, spectral_imaginary = inputs
        real_part = jnp.dot(spectral_real, reflectivity_real, preferred_element_type=jnp.float32) + jnp.dot(spectral_imaginary, reflectivity_imaginary, preferred_element_type=jnp.float32)
        imag_part = jnp.dot(spectral_imaginary, reflectivity_real, preferred_element_type=jnp.float32) - jnp.dot(spectral_real, reflectivity_imaginary, preferred_element_type=jnp.float32)
        return jnp.stack([real_part, imag_part]).astype(jnp.bfloat16)
    stacked = lax.map(single, (reflection[0], reflection[1], fourier_spectrum[0], fourier_spectrum[1]))
    return jnp.transpose(stacked, (1, 0, 2, 3))


def reference(reflection, direct, onset_index):
    cosine, sine_table = tables()
    samples = jnp.arange(NT, dtype=jnp.int32)
    window = (samples[None, None, :] < onset_index[:, :, None]).astype(jnp.float32)
    plus_field = direct
    minus_field = jnp.zeros_like(direct)
    for _ in range(ITERS):
        image = forward_apply(reflection, to_spectrum(plus_field, cosine, sine_table))
        minus_field = window * to_time(image, cosine, sine_table)
        back_image = adjoint_apply(reflection, to_spectrum(minus_field, cosine, sine_table))
        plus_field = direct + window * to_time(back_image, cosine, sine_table)
    return plus_field, minus_field
```

```python
import functools
import math

import jax
import jax.numpy as jnp
from jax import lax
from jax.experimental import pallas as pl
from jax.experimental.pallas import tpu as pltpu
from jax.sharding import PartitionSpec as P

NF = 96
NT = 512
FLO = 8
ITERS = 3
HIER = False
GROUPS = 1
VMEM = 48 * 1024 * 1024


def tables(bands):
    samples = jnp.arange(NT, dtype=jnp.int32)
    bins = FLO + jnp.arange(NF, dtype=jnp.int32)
    phase = bins[:, None] * samples[None, :] % NT
    angles = phase.astype(jnp.float32) * (2.0 * math.pi / NT)
    both = jnp.stack([jnp.cos(angles), -jnp.sin(angles)])
    return both.reshape(2, bands, NF // bands, NT).astype(jnp.bfloat16)


def forward_kernel(r_ref, g_ref, u_ref):
    parts, half = g_ref.shape[0], g_ref.shape[2] // 2
    g = jnp.concatenate([g_ref[j, 0] for j in range(parts)], axis=1)
    dims = (((1,), (1,)), ((), ()))
    a = lax.dot_general(g, r_ref[0, 0], dims, preferred_element_type=jnp.float32)
    b = lax.dot_general(g, r_ref[1, 0], dims, preferred_element_type=jnp.float32)
    u = jnp.concatenate([a[:half] - b[half:], a[half:] + b[:half]], axis=0)
    u_ref[0] = u.astype(u_ref.dtype)


def adjoint_kernel(r_ref, m_ref, w_ref):
    parts, half, width = w_ref.shape[0], w_ref.shape[2] // 2, w_ref.shape[3]
    m = m_ref[0]
    a = jnp.dot(m, r_ref[0, 0], preferred_element_type=jnp.float32)
    b = jnp.dot(m, r_ref[1, 0], preferred_element_type=jnp.float32)
    w = jnp.concatenate([a[:half] + b[half:], a[half:] - b[:half]], axis=0).astype(w_ref.dtype)
    for j in range(parts):
        w_ref[j, 0] = w[:, j * width:(j + 1) * width]


def multiply(kernel, refl, x, out_parts):
    _, bins, rows_s, cols = refl.shape
    lines, width = x.shape[-2:]
    if out_parts:
        x_spec = pl.BlockSpec((1, lines, width), lambda k: (k, 0, 0))
        o_shape = (out_parts, bins, lines, cols // out_parts)
        o_spec = pl.BlockSpec((out_parts, 1, lines, cols // out_parts), lambda k: (0, k, 0, 0))
    else:
        x_spec = pl.BlockSpec((x.shape[0], 1, lines, width), lambda k: (0, k, 0, 0))
        o_shape = (bins, lines, rows_s)
        o_spec = pl.BlockSpec((1, lines, rows_s), lambda k: (k, 0, 0))
    return pl.pallas_call(
        kernel,
        grid=(bins,),
        in_specs=[pl.BlockSpec((2, 1, rows_s, cols), lambda k: (0, k, 0, 0)), x_spec],
        out_specs=o_spec,
        out_shape=jax.ShapeDtypeStruct(o_shape, jnp.bfloat16),
        compiler_params=pltpu.CompilerParams(vmem_limit_bytes=VMEM),
        cost_estimate=pl.CostEstimate(
            flops=8 * bins * lines * rows_s * cols // 2,
            bytes_accessed=4 * bins * rows_s * cols,
            transcendentals=0,
        ),
    )(refl, x)


def to_bands(field, table, bands):
    spec = jnp.einsum("cbkt,pst->bkcps", table, field.astype(jnp.bfloat16), preferred_element_type=jnp.float32)
    spec = lax.all_to_all(spec.astype(jnp.bfloat16), "freq", split_axis=0, concat_axis=0, tiled=True)
    bands, bins, _, focal, width = spec.shape
    return spec.transpose(1, 2, 0, 3, 4).reshape(bins, 2 * bands * focal, width)


def to_trace(image, table, bands):
    bins, lines, width = image.shape
    spec = image.reshape(bins, 2, bands, lines // (2 * bands), width).transpose(2, 0, 1, 3, 4)
    spec = lax.all_to_all(spec, "freq", split_axis=0, concat_axis=0, tiled=True)
    return (2.0 / NT) * jnp.einsum("cbkt,bkcps->pst", table, spec, preferred_element_type=jnp.float32)


def gather(x, n):
    if not HIER:
        return lax.all_gather(x, "rcv", axis=0)
    same = [[2 * i + c for i in range(n // 2)] for c in range(2)]
    pairs = [[2 * i, 2 * i + 1] for i in range(n // 2)]
    y = lax.all_gather(x, "rcv", axis=0, axis_index_groups=pairs)
    y = lax.all_gather(y, "rcv", axis=0, axis_index_groups=[[2 * i + c for i in range(n // 2)] for c in range(2)])
    return y.reshape((n,) + x.shape)


def scatter(x, n):
    return lax.psum_scatter(x, "rcv", scatter_dimension=0, tiled=True).reshape(x.shape[1:])


def local(bands, parts, reflection, direct, onset_index):
    table = tables(bands)
    samples = jnp.arange(NT, dtype=jnp.int32)
    focal = direct.shape[0]
    cuts = [focal * i // GROUPS for i in range(GROUPS + 1)]
    fields = [direct[a:b] for a, b in zip(cuts, cuts[1:])]
    ons = [onset_index[a:b] for a, b in zip(cuts, cuts[1:])]
    plus, minus = list(fields), list(fields)
    for _ in range(ITERS):
        for i in range(GROUPS):
            inside = samples[None, None, :] < ons[i][:, :, None]
            g = gather(to_bands(plus[i], table, bands), parts)
            u = multiply(forward_kernel, reflection, g, 0)
            minus[i] = jnp.where(inside, to_trace(u, table, bands), 0.0)
        for i in range(GROUPS):
            inside = samples[None, None, :] < ons[i][:, :, None]
            m = to_bands(minus[i], table, bands)
            w = scatter(multiply(adjoint_kernel, reflection, m, parts), parts)
            plus[i] = fields[i] + jnp.where(inside, to_trace(w, table, bands), 0.0)
    if GROUPS == 1:
        return plus[0], minus[0]
    return jnp.concatenate(plus), jnp.concatenate(minus)


def solution(mesh):
    placed = (P(None, "freq", "rcv", None), P("freq", "rcv", None), P("freq", "rcv"))
    return jax.shard_map(
        functools.partial(local, mesh.shape["freq"], mesh.shape["rcv"]),
        mesh=mesh,
        in_specs=placed,
        out_specs=(P("freq", "rcv", None), P("freq", "rcv", None)),
        check_vma=False,
    )
```

```python
import functools
import math

import jax
import jax.numpy as jnp
from jax import lax
from jax.experimental import pallas as pl
from jax.experimental.pallas import tpu as pltpu
from jax.sharding import PartitionSpec as P

NF = 96
NT = 512
FLO = 8
ITERS = 3
GROUPS = 1
VMEM = 48 * 1024 * 1024


def tables(bands):
    samples = jnp.arange(NT, dtype=jnp.int32)
    bins = FLO + jnp.arange(NF, dtype=jnp.int32)
    phase = bins[:, None] * samples[None, :] % NT
    angles = phase.astype(jnp.float32) * (2.0 * math.pi / NT)
    both = jnp.stack([jnp.cos(angles), -jnp.sin(angles)])
    return both.reshape(2, bands, NF // bands, NT).astype(jnp.bfloat16)


def forward_kernel(r_ref, g_ref, u_ref):
    parts, half = g_ref.shape[0], g_ref.shape[2] // 2
    g = jnp.concatenate([g_ref[j, 0] for j in range(parts)], axis=1)
    dims = (((1,), (1,)), ((), ()))
    a = lax.dot_general(r_ref[0, 0], g, dims, preferred_element_type=jnp.float32).T
    b = lax.dot_general(r_ref[1, 0], g, dims, preferred_element_type=jnp.float32).T
    u = jnp.concatenate([a[:half] - b[half:], a[half:] + b[:half]], axis=0)
    u_ref[0] = u.astype(u_ref.dtype)


def adjoint_kernel(r_ref, m_ref, w_ref):
    parts, half, width = w_ref.shape[0], w_ref.shape[2] // 2, w_ref.shape[3]
    m = m_ref[0]
    a = jnp.dot(m, r_ref[0, 0], preferred_element_type=jnp.float32)
    b = jnp.dot(m, r_ref[1, 0], preferred_element_type=jnp.float32)
    w = jnp.concatenate([a[:half] + b[half:], a[half:] - b[:half]], axis=0).astype(w_ref.dtype)
    for j in range(parts):
        w_ref[j, 0] = w[:, j * width:(j + 1) * width]


def multiply(kernel, refl, x, out_parts):
    _, bins, rows_s, cols = refl.shape
    lines, width = x.shape[-2:]
    if out_parts:
        x_spec = pl.BlockSpec((1, lines, width), lambda k: (k, 0, 0))
        o_shape = (out_parts, bins, lines, cols // out_parts)
        o_spec = pl.BlockSpec((out_parts, 1, lines, cols // out_parts), lambda k: (0, k, 0, 0))
    else:
        x_spec = pl.BlockSpec((x.shape[0], 1, lines, width), lambda k: (0, k, 0, 0))
        o_shape = (bins, lines, rows_s)
        o_spec = pl.BlockSpec((1, lines, rows_s), lambda k: (k, 0, 0))
    return pl.pallas_call(
        kernel,
        grid=(bins,),
        in_specs=[pl.BlockSpec((2, 1, rows_s, cols), lambda k: (0, k, 0, 0)), x_spec],
        out_specs=o_spec,
        out_shape=jax.ShapeDtypeStruct(o_shape, jnp.bfloat16),
        compiler_params=pltpu.CompilerParams(vmem_limit_bytes=VMEM),
        cost_estimate=pl.CostEstimate(
            flops=8 * bins * lines * rows_s * cols // 2,
            bytes_accessed=4 * bins * rows_s * cols,
            transcendentals=0,
        ),
    )(refl, x)


def exchange_kernel(n, x_ref, o_ref, send_sem, recv_sem, own_sem):
    me = lax.axis_index("freq")
    barrier = pltpu.get_barrier_semaphore()
    for d in range(1, n):
        pl.semaphore_signal(
            barrier, inc=1, device_id={"freq": lax.rem(me + d, n)}, device_id_type=pl.DeviceIdType.MESH
        )
    pl.semaphore_wait(barrier, n - 1)
    copies = []
    for d in range(1, n):
        to = lax.rem(me + d, n)
        copies.append(
            pltpu.make_async_remote_copy(
                src_ref=x_ref.at[to],
                dst_ref=o_ref.at[me],
                send_sem=send_sem.at[d - 1],
                recv_sem=recv_sem.at[d - 1],
                device_id={"freq": to},
                device_id_type=pl.DeviceIdType.MESH,
            )
        )
    copies.append(pltpu.make_async_copy(x_ref.at[me], o_ref.at[me], own_sem))
    for copy in copies:
        copy.start()
    for copy in copies:
        copy.wait()


def exchange(x):
    n = x.shape[0]
    return pl.pallas_call(
        functools.partial(exchange_kernel, n),
        out_shape=jax.ShapeDtypeStruct(x.shape, x.dtype),
        in_specs=[pl.BlockSpec(memory_space=pltpu.VMEM)],
        out_specs=pl.BlockSpec(memory_space=pltpu.VMEM),
        scratch_shapes=[
            pltpu.SemaphoreType.DMA((n - 1,)),
            pltpu.SemaphoreType.DMA((n - 1,)),
            pltpu.SemaphoreType.DMA,
        ],
        compiler_params=pltpu.CompilerParams(collective_id=0, has_side_effects=True, vmem_limit_bytes=16 * 1024 * 1024),
    )(x)


def to_bands(field, table, bands):
    spec = jnp.einsum("cbkt,pst->bcpks", table, field.astype(jnp.bfloat16), preferred_element_type=jnp.float32)
    _, _, focal, bins, width = spec.shape
    spec = exchange(spec.astype(jnp.bfloat16).reshape(bands, -1, width))
    spec = spec.reshape(bands, 2, focal, bins, width)
    return spec.transpose(3, 1, 0, 2, 4).reshape(bins, 2 * bands * focal, width)


def to_trace(image, table, bands):
    bins, lines, width = image.shape
    focal = lines // (2 * bands)
    spec = image.reshape(bins, 2, bands, focal, width).transpose(2, 1, 3, 0, 4)
    spec = exchange(spec.reshape(bands, -1, width)).reshape(bands, 2, focal, bins, width)
    return (2.0 / NT) * jnp.einsum("cbkt,bcpks->pst", table, spec, preferred_element_type=jnp.float32)


def reach(rows, axis_device):
    barrier = pltpu.get_barrier_semaphore()
    for to in axis_device:
        pl.semaphore_signal(barrier, inc=1, device_id={"rcv": to}, device_id_type=pl.DeviceIdType.MESH)
    pl.semaphore_wait(barrier, rows)


def remote(src, dst, send_sem, recv_sem, to):
    return pltpu.make_async_remote_copy(
        src_ref=src, dst_ref=dst, send_sem=send_sem, recv_sem=recv_sem,
        device_id={"rcv": to}, device_id_type=pl.DeviceIdType.MESH,
    )


def gather_kernel(n, x_ref, o_ref, send_sem, recv_sem, own_sem):
    me, chips = lax.axis_index("rcv"), n // 2
    chip, core = me // 2, lax.rem(me, 2)
    sibling = 2 * chip + 1 - core
    peers = [2 * lax.rem(chip + d, chips) + core for d in range(1, chips)]
    reach(chips, peers + [sibling])
    direct = []
    for i, to in enumerate(peers + [sibling]):
        direct.append(remote(x_ref, o_ref.at[me], send_sem.at[i], recv_sem.at[i], to))
        direct[-1].start()
    own = pltpu.make_async_copy(x_ref, o_ref.at[me], own_sem)
    own.start()
    passed = []
    for d in range(1, chips):
        direct[d - 1].wait_recv()
        slot = 2 * lax.rem(chip - d + chips, chips) + core
        at = chips - 1 + d
        passed.append(remote(o_ref.at[slot], o_ref.at[slot], send_sem.at[at], recv_sem.at[at], sibling))
        passed[-1].start()
    direct[-1].wait_recv()
    for copy in direct:
        copy.wait_send()
    for copy in passed:
        copy.wait()
    own.wait()


def scatter_kernel(n, x_ref, o_ref, pair, held, landed, total, pair_send, pair_recv, send_sem, recv_sem):
    me, chips = lax.axis_index("rcv"), n // 2
    chip, core = me // 2, lax.rem(me, 2)
    sibling = 2 * chip + 1 - core
    bins = o_ref.shape[0]
    targets = [lax.rem(chip + d, chips) for d in range(1, chips + 1)]
    reach(chips, [2 * to + core for to in targets[:-1]] + [sibling])
    across = []
    for i, to in enumerate(targets):
        across.append(remote(x_ref.at[2 * to + 1 - core], pair.at[i], pair_send.at[i], pair_recv.at[i], sibling))
        across[-1].start()
    sent = []
    for i, to in enumerate(targets):
        across[i].wait_recv()
        last = i == chips - 1

        def add(k, carry, i=i, to=to, last=last):
            value = x_ref[2 * to + core, k].astype(jnp.float32) + pair[i, k].astype(jnp.float32)
            if last:
                total[k] = value
            else:
                held[i, k] = value.astype(held.dtype)
            return carry

        lax.fori_loop(0, bins, add, 0)
        if not last:
            sent.append(remote(held.at[i], landed.at[i], send_sem.at[i], recv_sem.at[i], 2 * to + core))
            sent[-1].start()
    for copy in sent:
        copy.wait_recv()

    def finish(k, carry):
        value = total[k]
        for i in range(chips - 1):
            value = value + landed[i, k].astype(jnp.float32)
        o_ref[k] = value.astype(o_ref.dtype)
        return carry

    lax.fori_loop(0, bins, finish, 0)
    for copy in sent + across:
        copy.wait_send()


def gather(x, n):
    sems = pltpu.SemaphoreType.DMA((n - 1,))
    return pl.pallas_call(
        functools.partial(gather_kernel, n),
        out_shape=jax.ShapeDtypeStruct((n,) + x.shape, x.dtype),
        in_specs=[pl.BlockSpec(memory_space=pltpu.VMEM)],
        out_specs=pl.BlockSpec(memory_space=pltpu.VMEM),
        scratch_shapes=[sems, sems, pltpu.SemaphoreType.DMA],
        compiler_params=pltpu.CompilerParams(collective_id=1, has_side_effects=True, vmem_limit_bytes=24 * 1024 * 1024),
    )(x)


def scatter(x, n):
    block = x.shape[1:]
    whole, rest = pltpu.SemaphoreType.DMA((n // 2,)), pltpu.SemaphoreType.DMA((n // 2 - 1,))
    return pl.pallas_call(
        functools.partial(scatter_kernel, n),
        out_shape=jax.ShapeDtypeStruct(block, x.dtype),
        in_specs=[pl.BlockSpec(memory_space=pltpu.VMEM)],
        out_specs=pl.BlockSpec(memory_space=pltpu.VMEM),
        scratch_shapes=[
            pltpu.VMEM((n // 2,) + block, x.dtype),
            pltpu.VMEM((n // 2 - 1,) + block, x.dtype),
            pltpu.VMEM((n // 2 - 1,) + block, x.dtype),
            pltpu.VMEM(block, jnp.float32),
            whole, whole, rest, rest,
        ],
        compiler_params=pltpu.CompilerParams(collective_id=2, has_side_effects=True, vmem_limit_bytes=32 * 1024 * 1024),
    )(x)


def local(bands, parts, reflection, direct, onset_index):
    table = tables(bands)
    samples = jnp.arange(NT, dtype=jnp.int32)
    focal = direct.shape[0]
    cuts = [focal * i // GROUPS for i in range(GROUPS + 1)]
    fields = [direct[a:b] for a, b in zip(cuts, cuts[1:])]
    ons = [onset_index[a:b] for a, b in zip(cuts, cuts[1:])]
    plus, minus = list(fields), list(fields)
    for _ in range(ITERS):
        for i in range(GROUPS):
            inside = samples[None, None, :] < ons[i][:, :, None]
            g = gather(to_bands(plus[i], table, bands), parts)
            u = multiply(forward_kernel, reflection, g, 0)
            minus[i] = jnp.where(inside, to_trace(u, table, bands), 0.0)
        for i in range(GROUPS):
            inside = samples[None, None, :] < ons[i][:, :, None]
            m = to_bands(minus[i], table, bands)
            w = scatter(multiply(adjoint_kernel, reflection, m, parts), parts)
            plus[i] = fields[i] + jnp.where(inside, to_trace(w, table, bands), 0.0)
    if GROUPS == 1:
        return plus[0], minus[0]
    return jnp.concatenate(plus), jnp.concatenate(minus)


def solution(mesh):
    placed = (P(None, "freq", "rcv", None), P("freq", "rcv", None), P("freq", "rcv"))
    return jax.shard_map(
        functools.partial(local, mesh.shape["freq"], mesh.shape["rcv"]),
        mesh=mesh,
        in_specs=placed,
        out_specs=(P("freq", "rcv", None), P("freq", "rcv", None)),
        check_vma=False,
    )
```
